512 devices in a mesh: dp: 32 (over y_lo, x, core), seq: 16 (over y_hi, z).
Axes of the slice: x: 4, y: 8 (y_hi: 2, y_lo: 4; y = y_hi * 4 + y_lo), z: 8, core: 2. Of those that a mesh axis runs over, the one named last changes fastest.
Arguments:
- queries: bfloat16 [32, 2048, 1536], P('dp', 'seq'), may hold values from -120 to 120
- keys: bfloat16 [32, 2048, 1536], P('dp', 'seq'), may hold values from -4.5 to 4.5
- values: bfloat16 [32, 2048, 1536], P('dp', 'seq'), may hold values from -6 to 6
- grad_out: bfloat16 [32, 2048, 1536], P('dp', 'seq'), may hold values from -6 to 6
- conv_weight: float32 [31, 1536], replicated, may hold values from -2 to 2
- conv_bias: float32 [1536], replicated, may hold values from -4 to 4
- lengths: int32 [32], P('dp'), may hold values from 512 to 2048, as said below
Outputs:
- query_grad: bfloat16 [32, 2048, 1536], P('dp', 'seq')
- key_grad: bfloat16 [32, 2048, 1536], P('dp', 'seq')
- value_grad: bfloat16 [32, 2048, 1536], P('dp', 'seq')
- weight_grad: float32 [31, 1536], P(None, 'seq')
- bias_grad: float32 [1536], P('seq')
The draws below stay inside these ranges and needn't reach their ends.
Inputs may be any that keep to these rules, and one draw needn't show every extreme that they name: `lengths`: each utterance's valid frames are its first ones; in every draw some utterance has all 2048 frames valid.
All inputs are finite; a program needn't handle non-finite values.
Results may differ from the reference program's by a relative error of at most 0.024.
Values may be sent and summed in bfloat16 or wider, within the bound.
A program may use at most 64 MiB of HBM per device.

```python
import math
import jax
import jax.numpy as jnp
from jax import lax

D = 1536
HEADS = 16
KERNEL = 31
UTTS = 32
LENGTH = 2048


def shared_keys(key):
    return jnp.clip(jax.random.normal(key, (UTTS, LENGTH, D), jnp.float32), -4.5, 4.5)


def draw_keys(key, part):
    base = shared_keys(key)
    return base.astype(jnp.bfloat16)


def draw_queries(key, part):
    key = jax.random.fold_in(key, 22)
    first = jax.random.fold_in(key, 0)
    drawn = 2.0 * jnp.clip(jax.random.normal(first, (UTTS, LENGTH, D), jnp.float32), -4.5, 4.5)
    return drawn.astype(jnp.bfloat16)


def draw_lengths(key, part):
    key = jax.random.fold_in(key, 3)
    first, second = jax.random.split(key)
    counts = jax.random.randint(first, (UTTS,), LENGTH // 4, LENGTH + 1, dtype=jnp.int32)
    full = jax.random.randint(second, (), 0, UTTS, dtype=jnp.int32)
    return jnp.where(jnp.arange(UTTS, dtype=jnp.int32) == full, LENGTH, counts).astype(jnp.int32)


def strengthened(values, stream_key, source, target, blocks, factor):
    owner, partner = [(jnp.arange(values.shape[axis_at]) // (values.shape[axis_at] // blocks)).reshape([-1 if axis == axis_at else 1 for axis in range(values.ndim)]) for axis_at in (source, target)]
    chosen = jax.random.permutation(stream_key, blocks)[partner]
    strong = (owner == chosen) | (owner == (partner + blocks // 2) % blocks)
    return jnp.where(strong, factor * values, values)


def levels(own_key, extent, cuts, smallest, high):
    level, own = 1.0, jax.random.fold_in(own_key, 6)
    for position, parts in cuts:
        steps = jnp.exp(jax.random.uniform(jax.random.fold_in(own, position), (parts,), jnp.float32, smallest / len(cuts), high / len(cuts)))
        level = level * jnp.repeat(steps, extent[position] // parts).reshape([-1 if axis == position else 1 for axis in range(len(extent))])
    return level


def centred(key, shape, scale, reach, pieces=(), kind=jnp.bfloat16):
    entries = jax.random.normal(key, shape, jnp.float32) * scale
    if len(pieces) > 0:
        entries = levels(key, shape, pieces, -0.22, 0.18) * entries
    return jnp.clip(entries, min=-reach, max=reach).astype(kind)


def gaussian_with(stream_key, dims, spread, most, pieces, heavy, kind=jnp.bfloat16):
    entries = spread * jax.random.normal(stream_key, dims, jnp.float32)
    if pieces:
        entries = entries * levels(stream_key, dims, pieces, -0.22, 0.18)
    return jnp.clip(strengthened(entries, jax.random.fold_in(stream_key, 3), *heavy), -most, most).astype(kind)


def setup_inputs(seed: int = 0) -> dict:
    key_of = jax.random.split(jax.random.key(seed), 8)
    queries = draw_queries(jax.random.fold_in(key_of[7], 71), 0)
    keys = draw_keys(jax.random.fold_in(key_of[7], 71), 0)
    values = centred(key_of[2], (UTTS, LENGTH, D), 1.0, 6.0, ((0, 32), (1, 16)))
    grad_out = gaussian_with(key_of[3], (UTTS, LENGTH, D), 1.0, 6.0, ((0, 32), (1, 16)), (1, 2, 16, 2.0))
    conv_weight = centred(key_of[4], (KERNEL, D), (KERNEL // 4) ** -0.5, 2.0, (), jnp.float32)
    conv_bias = centred(key_of[5], (D,), 1.0, 4.0, (), jnp.float32)
    lengths = draw_lengths(jax.random.fold_in(key_of[7], 71), 0)
    return {"queries": queries, "keys": keys, "values": values, "grad_out": grad_out, "conv_weight": conv_weight, "conv_bias": conv_bias, "lengths": lengths}


masked_score = -1e+30

def rounded(array):
    return lax.optimization_barrier(array.astype(jnp.bfloat16)).astype(jnp.float32)

def probs_rows(query_block, key_all, key_valid, score_scale):
    scores = jnp.einsum('qhd,khd->hqk', query_block, key_all) * score_scale
    scores = jnp.where(key_valid[None, None, :], scores, masked_score)
    row_top = lax.optimization_barrier(jnp.max(scores, axis=-1, keepdims=True))
    exped = jnp.exp(scores - row_top)
    return exped / lax.optimization_barrier(jnp.sum(exped, axis=-1, keepdims=True))

def utterance(query, keyin, value, grad, length, weight, bias):
    seq_len, width = query.shape
    head_dim = width // HEADS
    rim = KERNEL // 2
    block_rows = math.gcd(seq_len, 512)
    count = seq_len // block_rows
    score_scale = 1.0 / math.sqrt(head_dim)
    valid = jnp.arange(seq_len, dtype=jnp.int32) < length
    query_f = query.astype(jnp.float32).reshape(seq_len, HEADS, head_dim)
    key_f = keyin.astype(jnp.float32).reshape(seq_len, HEADS, head_dim)
    value_f = value.astype(jnp.float32).reshape(seq_len, HEADS, head_dim)
    query_blocks = query_f.reshape(count, block_rows, HEADS, head_dim)

    def block_out(query_block):
        probs = probs_rows(query_block, key_f, valid, score_scale)
        return jnp.einsum('hqk,khd->qhd', rounded(probs), value_f)
    attended = lax.map(block_out, query_blocks).reshape(seq_len, width)
    attended = rounded(attended * valid[:, None].astype(jnp.float32))
    padded = jnp.pad(attended, ((rim, rim), (0, 0)))
    conv_pre = jnp.zeros((seq_len, width), jnp.float32) + bias
    for j in range(KERNEL):
        conv_pre = conv_pre + weight[j] * padded[j:j + seq_len]
    sig = jax.nn.sigmoid(conv_pre)
    pre_grad = rounded(grad.astype(jnp.float32) * sig * (1.0 + conv_pre * (1.0 - sig)))
    weight_part = jnp.stack([lax.optimization_barrier(jnp.sum(pre_grad * padded[j:j + seq_len], axis=0)) for j in range(KERNEL)])
    bias_part = lax.optimization_barrier(jnp.sum(pre_grad, axis=0))
    grad_pad = jnp.pad(pre_grad, ((rim, rim), (0, 0)))
    attn_grad = grad.astype(jnp.float32)
    for j in range(KERNEL):
        attn_grad = attn_grad + weight[j] * grad_pad[2 * rim - j:2 * rim - j + seq_len]
    attn_grad = rounded(attn_grad * valid[:, None].astype(jnp.float32))
    grad_blocks = attn_grad.reshape(count, block_rows, HEADS, head_dim)

    def block_step(carry, inputs):
        key_acc, value_acc = carry
        query_block, grad_block = inputs
        probs = probs_rows(query_block, key_f, valid, score_scale)
        score_grad = jnp.einsum('qhd,khd->hqk', grad_block, value_f)
        row_delta = lax.optimization_barrier(jnp.sum(probs * score_grad, axis=-1, keepdims=True))
        diff = rounded(probs * (score_grad - row_delta))
        query_part = (jnp.einsum('hqk,khd->qhd', diff, key_f) * score_scale).astype(jnp.bfloat16)
        key_acc = key_acc + jnp.einsum('hqk,qhd->khd', diff, query_block)
        value_acc = value_acc + jnp.einsum('hqk,qhd->khd', rounded(probs), grad_block)
        return ((key_acc, value_acc), query_part)
    zeros = jnp.zeros((seq_len, HEADS, head_dim), jnp.float32)
    (key_acc, value_acc), query_parts = lax.scan(block_step, (zeros, zeros), (query_blocks, grad_blocks))
    query_out = query_parts.reshape(seq_len, width)
    key_out = (key_acc * score_scale).astype(jnp.bfloat16).reshape(seq_len, width)
    value_out = value_acc.astype(jnp.bfloat16).reshape(seq_len, width)
    return (query_out, key_out, value_out, weight_part, bias_part)

def reference(queries, keys, values, grad_out, conv_weight, conv_bias, lengths):

    def per_utterance(inputs):
        query, keyin, value, grad, length = inputs
        return utterance(query, keyin, value, grad, length, conv_weight, conv_bias)
    query_grad, key_grad, value_grad, weight_parts, bias_parts = lax.map(per_utterance, (queries, keys, values, grad_out, lengths))
    return (query_grad, key_grad, value_grad, lax.optimization_barrier(jnp.sum(weight_parts, axis=0)), lax.optimization_barrier(jnp.sum(bias_parts, axis=0)))
```

```python
import math

import jax
import jax.numpy as jnp
from jax import lax
from jax.experimental import pallas as pl
from jax.experimental.pallas import tpu as pltpu
from jax.sharding import PartitionSpec as P

MESH = pl.DeviceIdType.MESH
HEADS = 16
KERNEL = 31
RIM = KERNEL // 2
HEAD = 96
WIDE = 128
PAD = 16
ROWS = 256
CONV = 128
NEG = -1e30
F32 = jnp.float32
BF16 = jnp.bfloat16
NT = (((1,), (1,)), ((), ()))


def core(
    q_hbm, k_hbm, v_hbm, g_hbm, weight_ref, bias_ref, length_ref,
    dq_ref, dk_ref, dv_ref, dw_ref, db_ref,
    raw, stage, q_t, k_t, v_t, g_t, weights, low, att, out_nat, slope, pre, upper,
    grad_x, grad_t, stage_out, back, tap_sum, one, two, three,
    load_sem, own_sem, send_sem, recv_sem, sum_send, sum_recv,
):
    seq_len = q_t.shape[1]
    frames = raw.shape[1]
    width = raw.shape[2]
    me = lax.axis_index("seq")
    dp = lax.axis_index("dp")
    dp_core = lax.rem(dp, 2)
    dp_x = lax.rem(dp // 2, 4)
    dp_y = dp // 8
    length = length_ref[0]

    sources = (k_hbm, q_hbm, v_hbm, g_hbm)
    loads = [
        pltpu.make_async_copy(ref.at[0], raw.at[i], load_sem.at[i])
        for i, ref in enumerate(sources)
    ]
    for load in loads:
        load.start()
    seq_peers = [lax.rem(me + step, HEADS) for step in range(1, HEADS)]
    core_peers = [dp_y * 8 + dp_x * 2 + 1 - dp_core]
    x_peers = [dp_y * 8 + lax.rem(dp_x + s, 4) * 2 + dp_core for s in (1, 2, 3)]
    y_peers = [lax.rem(dp_y + s, 4) * 8 + dp_x * 2 + dp_core for s in (1, 2, 3)]
    barrier = pltpu.get_barrier_semaphore()
    for peer in seq_peers:
        pl.semaphore_signal(barrier, inc=1, device_id={"seq": peer}, device_id_type=MESH)
    for peer in core_peers + x_peers + y_peers:
        pl.semaphore_signal(barrier, inc=1, device_id={"dp": peer}, device_id_type=MESH)

    k_t[HEAD:, :] = jnp.zeros((WIDE - HEAD, seq_len), BF16)
    key_pos = lax.broadcasted_iota(jnp.int32, (16, seq_len), 1)
    key_row = lax.broadcasted_iota(jnp.int32, (16, seq_len), 0)
    mask = jnp.where((key_row == 0) & (key_pos >= length), F32(NEG), F32(0.0))
    k_t[HEAD : HEAD + 16, :] = mask.astype(BF16)
    q_t[HEAD:, :] = jnp.zeros((WIDE - HEAD, seq_len), BF16)
    q_t[HEAD : HEAD + 16, :] = jnp.where(key_row == 0, F32(1.0), F32(0.0)).astype(BF16)
    v_t[HEAD:, :] = jnp.zeros((WIDE - HEAD, seq_len), BF16)
    v_t[HEAD : HEAD + 16, :] = jnp.where(key_row < 3, F32(1.0), F32(0.0)).astype(BF16)
    g_t[HEAD:, :] = jnp.zeros((WIDE - HEAD, seq_len), BF16)
    first = pl.multiple_of((me * HEAD) // WIDE * WIDE, WIDE)
    second = pl.multiple_of(jnp.minimum((me * HEAD) // WIDE + 1, width // WIDE - 1) * WIDE, WIDE)

    def own_columns(ref):
        both = jnp.concatenate([ref[:, pl.ds(first, WIDE)], ref[:, pl.ds(second, WIDE)]], axis=1)
        part = both[:, 0:HEAD]
        for turn in range(1, 4):
            at = turn * HEAD % WIDE
            part = jnp.where(lax.rem(me, 4) == turn, both[:, at : at + HEAD], part)
        return part

    weights[...] = jnp.zeros(weights.shape, F32)
    weights[0:KERNEL, 0:HEAD] = own_columns(weight_ref)
    weights[KERNEL : KERNEL + 1, 0:HEAD] = own_columns(bias_ref)
    zero_rim = jnp.zeros((PAD, WIDE), F32)
    for buffer in (att, pre):
        buffer[0:PAD, :] = zero_rim
        buffer[PAD + seq_len :, :] = zero_rim
    tap_sum[...] = jnp.zeros(tap_sum.shape, F32)

    pl.semaphore_wait(barrier, 2 * HEADS - 10)

    own_lanes = pl.ds(pl.multiple_of(me * frames, frames), frames)
    own_rows = pl.ds(pl.multiple_of(me * HEAD, HEAD), HEAD)
    landings = (k_t, q_t, v_t, g_t)
    kept = []
    for i, landing in enumerate(landings):
        loads[i].wait()
        for b in range(width // WIDE):
            stage[i, b * WIDE : (b + 1) * WIDE, :] = raw[i, :, b * WIDE : (b + 1) * WIDE].T
        target = landing.at[pl.ds(0, HEAD), own_lanes]
        for peer in seq_peers:
            pltpu.make_async_remote_copy(
                src_ref=stage.at[i, pl.ds(pl.multiple_of(peer * HEAD, HEAD), HEAD), :],
                dst_ref=target,
                send_sem=send_sem.at[i],
                recv_sem=recv_sem.at[i],
                device_id={"seq": peer},
                device_id_type=MESH,
            ).start()
        keep = pltpu.make_async_copy(stage.at[i, own_rows, :], target, own_sem.at[i])
        keep.start()
        kept.append(keep)

    def arrived(i):
        kept[i].wait()
        whole = landings[i].at[pl.ds(0, HEAD), pl.ds(0, seq_len - frames)]
        pltpu.make_async_copy(whole, whole, recv_sem.at[i]).wait()

    arrived(0)
    arrived(1)
    arrived(2)

    rate = F32(math.log2(math.e) / math.sqrt(HEAD))

    def forward(step, _):
        at = pl.multiple_of(step * ROWS, ROWS)
        rows = pl.ds(at, ROWS)
        query = q_t[:, rows].T
        scores = jnp.dot(query, k_t[...], preferred_element_type=F32)
        top = jnp.max(scores, axis=1, keepdims=True)
        exped = jnp.exp2((scores - top) * rate).astype(BF16)
        low[rows, :] = exped
        out_t = lax.dot_general(v_t[...], exped, NT, preferred_element_type=F32)
        out = out_t.T
        total = out[:, HEAD : HEAD + 1]
        upper[rows, :] = jnp.broadcast_to(1.0 / total, (ROWS, WIDE))
        out = out * (1.0 / total)
        out_nat[rows, :] = out
        place = at + lax.broadcasted_iota(jnp.int32, (ROWS, WIDE), 0)
        lane = lax.broadcasted_iota(jnp.int32, (ROWS, WIDE), 1)
        shown = jnp.where((place < length) & (lane < HEAD), out, 0.0)
        att[pl.ds(pl.multiple_of(PAD + at, PAD), ROWS), :] = shown.astype(BF16).astype(F32)
        return 0

    lax.fori_loop(0, seq_len // ROWS, forward, 0)

    def conv(step, _):
        at = pl.multiple_of(step * CONV, CONV)
        window = att[pl.ds(at, CONV + 2 * PAD), :]
        total = jnp.broadcast_to(weights[KERNEL : KERNEL + 1, :], (CONV, WIDE))
        for j in range(KERNEL):
            total = total + weights[j : j + 1, :] * window[j + 1 : j + 1 + CONV, :]
        sig = jax.nn.sigmoid(total)
        slope[pl.ds(at, CONV), :] = sig * (1.0 + total * (1.0 - sig))
        return 0

    lax.fori_loop(0, seq_len // CONV, conv, 0)
    arrived(3)

    def gate(step, _):
        at = pl.multiple_of(step * CONV, CONV)
        rows = pl.ds(at, CONV)
        grad = g_t[:, rows].T.astype(F32)
        gated = (grad * slope[rows, :]).astype(BF16).astype(F32)
        pre[pl.ds(pl.multiple_of(PAD + at, PAD), CONV), :] = gated
        return 0

    lax.fori_loop(0, seq_len // CONV, gate, 0)

    def conv_back(step, _):
        at = pl.multiple_of(step * CONV, CONV)
        rows = pl.ds(at, CONV)
        window = pre[pl.ds(at, CONV + 2 * PAD), :]
        total = g_t[:, rows].T.astype(F32)
        for j in range(KERNEL):
            shift = PAD + RIM - j
            total = total + weights[j : j + 1, :] * window[shift : shift + CONV, :]
        place = at + lax.broadcasted_iota(jnp.int32, (CONV, WIDE), 0)
        lane = lax.broadcasted_iota(jnp.int32, (CONV, WIDE), 1)
        total = jnp.where((place < length) & (lane < HEAD), total, 0.0).astype(BF16).astype(F32)
        scaled = (total * upper[rows, :]).astype(BF16).astype(F32)
        delta = -jnp.sum(scaled * out_nat[rows, :], axis=1, keepdims=True)
        high = delta.astype(BF16).astype(F32)
        middle = (delta - high).astype(BF16).astype(F32)
        last = delta - high - middle
        scaled = jnp.where(lane == HEAD, high, scaled)
        scaled = jnp.where(lane == HEAD + 1, middle, scaled)
        scaled = jnp.where(lane == HEAD + 2, last, scaled).astype(BF16)
        grad_x[rows, :] = scaled
        grad_t[:, rows] = scaled.T
        return 0

    lax.fori_loop(0, seq_len // CONV, conv_back, 0)

    out_sent = [len(landings) + i for i in range(3)]

    def send_back(which, step):
        for part in range(ROWS // frames):
            peer = step * (ROWS // frames) + part
            source = stage_out.at[which, pl.ds(pl.multiple_of(peer * HEAD, HEAD), HEAD), :]
            target = back.at[which, own_rows, :]

            @pl.when(peer != me)
            def _():
                pltpu.make_async_remote_copy(
                    src_ref=source,
                    dst_ref=target,
                    send_sem=send_sem.at[out_sent[which]],
                    recv_sem=recv_sem.at[out_sent[which]],
                    device_id={"seq": peer},
                    device_id_type=MESH,
                ).start()

    def put(which, step, block):
        for part in range(ROWS // frames):
            peer = step * (ROWS // frames) + part
            piece = block[:, part * frames : (part + 1) * frames]
            stage_out[which, pl.ds(pl.multiple_of(peer * HEAD, HEAD), HEAD), :] = piece
        send_back(which, step)

    steps = seq_len // ROWS
    turned = me // (ROWS // frames)

    def value_step(step, _):
        step = lax.rem(step + turned, steps)
        columns = pl.ds(pl.multiple_of(step * ROWS, ROWS), ROWS)
        block = jnp.dot(grad_t[0:HEAD, :], low[:, columns], preferred_element_type=F32)
        put(2, step, block.astype(BF16))
        return 0

    lax.fori_loop(0, steps, value_step, 0)

    def taps(step, _):
        at = pl.multiple_of(step * CONV, CONV)
        window = att[pl.ds(at, CONV + 2 * PAD), :]
        gated = pre[pl.ds(pl.multiple_of(PAD + at, PAD), CONV), :]
        for j in range(KERNEL):
            term = gated * window[j + 1 : j + 1 + CONV, :]
            tap_sum[j] += jnp.sum(term.reshape(CONV // 8, 8, WIDE), axis=0)
        tap_sum[KERNEL] += jnp.sum(gated.reshape(CONV // 8, 8, WIDE), axis=0)
        return 0

    lax.fori_loop(0, seq_len // CONV, taps, 0)

    def sum_start(level, slots, mine, peers, value):
        slots[mine] = value
        for peer in peers:
            pltpu.make_async_remote_copy(
                src_ref=slots.at[mine],
                dst_ref=slots.at[mine],
                send_sem=sum_send.at[level],
                recv_sem=sum_recv.at[level],
                device_id={"dp": peer},
                device_id_type=MESH,
            ).start()

    def sum_end(level, slots, peers):
        whole = slots.at[pl.ds(0, len(peers))]
        pltpu.make_async_copy(whole, whole, sum_recv.at[level]).wait()
        value = slots[0]
        for i in range(1, len(peers) + 1):
            value = value + slots[i]
        return value

    sum_start(0, one, dp_core, core_peers, jnp.sum(tap_sum[...], axis=1))

    back_scale = F32(1.0 / math.sqrt(HEAD))

    def query_step(step, _):
        step = lax.rem(step + turned, steps)
        rows = pl.ds(pl.multiple_of(step * ROWS, ROWS), ROWS)
        change = jnp.dot(grad_x[rows, :], v_t[...], preferred_element_type=F32)
        diff = (change * low[rows, :].astype(F32)).astype(BF16)
        low[rows, :] = diff
        block = lax.dot_general(k_t[0:HEAD, :], diff, NT, preferred_element_type=F32)
        put(0, step, (block * back_scale).astype(BF16))
        return 0

    lax.fori_loop(0, steps, query_step, 0)
    sum_start(1, two, dp_x, x_peers, sum_end(0, one, core_peers))

    def key_step(step, _):
        step = lax.rem(step + turned, steps)
        columns = pl.ds(pl.multiple_of(step * ROWS, ROWS), ROWS)
        block = jnp.dot(q_t[0:HEAD, :], low[:, columns], preferred_element_type=F32)
        put(1, step, (block * back_scale).astype(BF16))
        return 0

    lax.fori_loop(0, steps, key_step, 0)
    sum_start(2, three, dp_y, y_peers, sum_end(1, two, x_peers))
    sums = sum_end(2, three, y_peers)
    dw_ref[...] = sums[0:KERNEL, 0:HEAD]
    db_ref[...] = sums[KERNEL : KERNEL + 1, 0:HEAD]

    others = pl.ds(0, (HEADS - 1) * HEAD)
    for which, result in ((2, dv_ref), (0, dq_ref), (1, dk_ref)):
        back[which, own_rows, :] = stage_out[which, own_rows, :]
        whole = back.at[which, others, :]
        pltpu.make_async_copy(whole, whole, recv_sem.at[out_sent[which]]).wait()
        for b in range(width // WIDE):
            result[0, :, b * WIDE : (b + 1) * WIDE] = back[which, b * WIDE : (b + 1) * WIDE, :].T
    for i in range(len(landings) + 3):
        whole = stage.at[0, others, :]
        pltpu.make_async_copy(whole, whole, send_sem.at[i]).wait()
    for level, (slots, peers) in enumerate(((one, core_peers), (two, x_peers), (three, y_peers))):
        whole = slots.at[pl.ds(0, len(peers))]
        pltpu.make_async_copy(whole, whole, sum_send.at[level]).wait()


def on_device(queries, keys, values, grad_out, conv_weight, conv_bias, lengths):
    _, frames, width = queries.shape
    seq_len = frames * HEADS
    any_spec = pl.BlockSpec(memory_space=pl.ANY)
    vmem = pl.BlockSpec(memory_space=pltpu.VMEM)
    block = jax.ShapeDtypeStruct(queries.shape, BF16)
    tall = seq_len + 2 * PAD
    query_grad, key_grad, value_grad, weight_grad, bias_grad = pl.pallas_call(
        core,
        out_shape=(
            block,
            block,
            block,
            jax.ShapeDtypeStruct((KERNEL, HEAD), F32),
            jax.ShapeDtypeStruct((1, HEAD), F32),
        ),
        in_specs=[any_spec] * 4 + [vmem, vmem, pl.BlockSpec(memory_space=pltpu.SMEM)],
        out_specs=(vmem,) * 5,
        scratch_shapes=[
            pltpu.VMEM((4, frames, width), BF16),
            pltpu.VMEM((4, width, frames), BF16),
            pltpu.VMEM((WIDE, seq_len), BF16),
            pltpu.VMEM((WIDE, seq_len), BF16),
            pltpu.VMEM((WIDE, seq_len), BF16),
            pltpu.VMEM((WIDE, seq_len), BF16),
            pltpu.VMEM((KERNEL + 1, WIDE), F32),
            pltpu.VMEM((seq_len, seq_len), BF16),
            pltpu.VMEM((tall, WIDE), F32),
            pltpu.VMEM((seq_len, WIDE), F32),
            pltpu.VMEM((seq_len, WIDE), F32),
            pltpu.VMEM((tall, WIDE), F32),
            pltpu.VMEM((seq_len, WIDE), F32),
            pltpu.VMEM((seq_len, WIDE), BF16),
            pltpu.VMEM((WIDE, seq_len), BF16),
            pltpu.VMEM((3, width, frames), BF16),
            pltpu.VMEM((3, width, frames), BF16),
            pltpu.VMEM((KERNEL + 1, 8, WIDE), F32),
            pltpu.VMEM((2, KERNEL + 1, WIDE), F32),
            pltpu.VMEM((4, KERNEL + 1, WIDE), F32),
            pltpu.VMEM((4, KERNEL + 1, WIDE), F32),
            pltpu.SemaphoreType.DMA((4,)),
            pltpu.SemaphoreType.DMA((4,)),
            pltpu.SemaphoreType.DMA((7,)),
            pltpu.SemaphoreType.DMA((7,)),
            pltpu.SemaphoreType.DMA((3,)),
            pltpu.SemaphoreType.DMA((3,)),
        ],
        compiler_params=pltpu.CompilerParams(
            collective_id=0, has_side_effects=True, vmem_limit_bytes=56 << 20
        ),
    )(queries, keys, values, grad_out, conv_weight, conv_bias[None, :], lengths)
    return query_grad, key_grad, value_grad, weight_grad, bias_grad[0]


def solution(mesh):
    return jax.shard_map(
        on_device,
        mesh=mesh,
        in_specs=(
            P("dp", "seq", None),
            P("dp", "seq", None),
            P("dp", "seq", None),
            P("dp", "seq", None),
            P(),
            P(),
            P("dp"),
        ),
        out_specs=(
            P("dp", "seq", None),
            P("dp", "seq", None),
            P("dp", "seq", None),
            P(None, "seq"),
            P("seq"),
        ),
        check_vma=False,
    )
```

```python
import math

import jax
import jax.numpy as jnp
from jax import lax
from jax.experimental import pallas as pl
from jax.experimental.pallas import tpu as pltpu
from jax.sharding import PartitionSpec as P

MESH = pl.DeviceIdType.MESH
HEADS = 16
KERNEL = 31
EARLY = False
HEAD = 96
WIDE = 128
PAD = 16
ROWS = 256
CONV = 128
NEG = -1e30
F32 = jnp.float32
BF16 = jnp.bfloat16


def core(
    q_hbm, k_hbm, v_hbm, g_hbm, weight_ref, bias_ref, length_ref,
    dq_ref, dk_ref, dv_ref, dw_ref, db_ref,
    raw, stage, q_t, k_t, v_t, g_t, weights, low, att, out_nat, slope, pre, upper,
    grad_x, grad_t, grad_nat, k_nat, v_nat, stage_out, back, done, tap_sum, one, two, three,
    load_sem, own_sem, send_sem, recv_sem, grad_sem, store_sem, sum_send, sum_recv,
):
    seq_len = q_t.shape[1]
    frames = raw.shape[1]
    width = raw.shape[2]
    me = lax.axis_index("seq")
    dp = lax.axis_index("dp")
    dp_core = lax.rem(dp, 2)
    dp_x = lax.rem(dp // 2, 4)
    dp_y = dp // 8
    length = length_ref[0]

    me_y, me_z = me // 8, lax.rem(me, 8)
    turns = [(dy, dz) for dz in (4, 3, 5, 2, 6, 1, 7, 0) for dy in (1, 0)][:-1]
    seq_peers = [lax.rem(me_y + dy, 2) * 8 + lax.rem(me_z + dz, 8) for dy, dz in turns]
    core_peers = [dp_y * 8 + dp_x * 2 + 1 - dp_core]
    x_peers = [dp_y * 8 + lax.rem(dp_x + s, 4) * 2 + dp_core for s in (1, 2, 3)]
    y_peers = [lax.rem(dp_y + s, 4) * 8 + dp_x * 2 + dp_core for s in (1, 2, 3)]
    barrier = pltpu.get_barrier_semaphore()
    for peer in seq_peers:
        pl.semaphore_signal(barrier, inc=1, device_id={"seq": peer}, device_id_type=MESH)
    for peer in core_peers + x_peers + y_peers:
        pl.semaphore_signal(barrier, inc=1, device_id={"dp": peer}, device_id_type=MESH)

    sources = (k_hbm, q_hbm, v_hbm, g_hbm)
    loads = [
        pltpu.make_async_copy(ref.at[0], raw.at[i], load_sem.at[i])
        for i, ref in enumerate(sources)
    ]
    for load in loads:
        load.start()

    own_lanes = pl.ds(pl.multiple_of(me * frames, frames), frames)
    own_rows = pl.ds(pl.multiple_of(me * HEAD, HEAD), HEAD)
    landings = (k_t, q_t, v_t, g_t)
    others = pl.ds(0, (HEADS - 1) * HEAD)

    early = EARLY

    def turn_around(i):
        loads[i].wait()
        for b in range(width // WIDE):
            stage[i, b * WIDE : (b + 1) * WIDE, :] = raw[i, :, b * WIDE : (b + 1) * WIDE].T

    def send(i):
        target = landings[i].at[pl.ds(0, HEAD), own_lanes]
        for peer in seq_peers:
            pltpu.make_async_remote_copy(
                src_ref=stage.at[i, pl.ds(pl.multiple_of(peer * HEAD, HEAD), HEAD), :],
                dst_ref=target,
                send_sem=send_sem.at[i],
                recv_sem=grad_sem.at[me] if i == 3 else recv_sem.at[i],
                device_id={"seq": peer},
                device_id_type=MESH,
            ).start()
        pltpu.make_async_copy(stage.at[i, own_rows, :], target, own_sem.at[i]).start()

    def sent(i):
        whole = stage.at[0, others, :]
        pltpu.make_async_copy(whole, whole, send_sem.at[i]).wait()

    def arrived(i):
        mine = stage.at[i, own_rows, :]
        pltpu.make_async_copy(mine, mine, own_sem.at[i]).wait()
        whole = landings[i].at[pl.ds(0, HEAD), pl.ds(0, seq_len - frames)]
        pltpu.make_async_copy(whole, whole, recv_sem.at[i]).wait()

    turn_around(0)
    turn_around(1)
    pl.semaphore_wait(barrier, len(seq_peers + core_peers + x_peers + y_peers))
    send(0)
    send(1)
    turn_around(2)
    send(2)
    turn_around(3)
    if not early:
        send(3)

    k_t[HEAD:, :] = jnp.zeros((WIDE - HEAD, seq_len), BF16)
    key_pos = lax.broadcasted_iota(jnp.int32, (16, seq_len), 1)
    key_row = lax.broadcasted_iota(jnp.int32, (16, seq_len), 0)
    mask = jnp.where((key_row == 0) & (key_pos >= length), F32(NEG), F32(0.0))
    k_t[HEAD : HEAD + 16, :] = mask.astype(BF16)
    q_t[HEAD:, :] = jnp.zeros((WIDE - HEAD, seq_len), BF16)
    q_t[HEAD : HEAD + 16, :] = jnp.where(key_row == 0, F32(1.0), F32(0.0)).astype(BF16)
    v_t[HEAD:, :] = jnp.zeros((WIDE - HEAD, seq_len), BF16)
    v_t[HEAD : HEAD + 16, :] = jnp.where(key_row < 3, F32(1.0), F32(0.0)).astype(BF16)
    g_t[HEAD:, :] = jnp.zeros((WIDE - HEAD, seq_len), BF16)
    first = pl.multiple_of((me * HEAD) // WIDE * WIDE, WIDE)
    second = pl.multiple_of(jnp.minimum((me * HEAD) // WIDE + 1, width // WIDE - 1) * WIDE, WIDE)

    def own_columns(ref):
        pair = [ref[..., pl.ds(first, WIDE)], ref[..., pl.ds(second, WIDE)]]
        both = jnp.concatenate([part.reshape(-1, WIDE) for part in pair], axis=1)
        part = both[:, 0:HEAD]
        for turn in range(1, 4):
            at = turn * HEAD % WIDE
            part = jnp.where(lax.rem(me, 4) == turn, both[:, at : at + HEAD], part)
        return part

    weights[...] = jnp.zeros(weights.shape, F32)
    own_taps = own_columns(weight_ref)
    for j in range(KERNEL):
        weights[j, :, 0:HEAD] = jnp.broadcast_to(own_taps[j : j + 1, :], (8, HEAD))
    weights[KERNEL, :, 0:HEAD] = jnp.broadcast_to(own_columns(bias_ref), (8, HEAD))
    zero_rim = jnp.zeros((PAD, WIDE), F32)
    for buffer in (att, pre):
        buffer[0:PAD, :] = zero_rim
        buffer[PAD + seq_len :, :] = zero_rim
    tap_sum[...] = jnp.zeros(tap_sum.shape, F32)

    arrived(0)
    arrived(1)

    rate = F32(math.log2(math.e) / math.sqrt(HEAD))
    steps = seq_len // ROWS

    def weigh(step, _):
        rows = pl.ds(pl.multiple_of(step * ROWS, ROWS), ROWS)
        query = q_t[:, rows].T
        scores = jnp.dot(query, k_t[...], preferred_element_type=F32)
        top = jnp.max(scores, axis=1, keepdims=True)
        low[rows, :] = jnp.exp2((scores - top) * rate).astype(BF16)
        return 0

    def forward(step, _):
        at = pl.multiple_of(step * ROWS, ROWS)
        rows = pl.ds(at, ROWS)
        out = jnp.dot(low[rows, :], v_nat[...], preferred_element_type=F32)
        inverse = 1.0 / out[:, HEAD : HEAD + 1]
        upper[rows, :] = jnp.broadcast_to(inverse, (ROWS, WIDE))
        out = out * inverse
        out_nat[rows, :] = out
        place = at + lax.broadcasted_iota(jnp.int32, (ROWS, WIDE), 0)
        lane = lax.broadcasted_iota(jnp.int32, (ROWS, WIDE), 1)
        shown = jnp.where((place < length) & (lane < HEAD), out, 0.0)
        att[pl.ds(pl.multiple_of(PAD + at, PAD), ROWS), :] = shown.astype(BF16).astype(F32)
        return 0

    def turn(wide_ref, tall_ref):
        for b in range(seq_len // WIDE):
            part = slice(b * WIDE, (b + 1) * WIDE)
            tall_ref[part, :] = wide_ref[:, part].T

    def shifts(buffer, at):
        window = buffer[pl.ds(at, CONV + 2 * PAD), :]
        return [window[r : r + CONV + 2 * PAD - 8, :] for r in range(8)]

    def moved(parts, offset):
        aligned = offset // 8 * 8
        part = parts[offset % 8][aligned : aligned + CONV, :]
        return part.reshape(CONV // 8, 8, WIDE)

    if early:
        sent(0)
        send(3)
    lax.fori_loop(0, steps, weigh, 0)
    turn(k_t, k_nat)
    arrived(2)
    turn(v_t, v_nat)
    lax.fori_loop(0, steps, forward, 0)

    by_shift = sorted(range(1, KERNEL + 1), key=lambda offset: offset % 8)

    def conv(step, _):
        at = pl.multiple_of(step * CONV, CONV)
        parts = shifts(att, at)
        total = jnp.broadcast_to(weights[KERNEL][None], (CONV // 8, 8, WIDE))
        for offset in by_shift:
            total = total + weights[offset - 1][None] * moved(parts, offset)
        total = total.reshape(CONV, WIDE)
        sig = jax.nn.sigmoid(total)
        slope[pl.ds(at, CONV), :] = sig * (1.0 + total * (1.0 - sig))
        return 0

    lax.fori_loop(0, seq_len // CONV, conv, 0)

    def rank(k):
        odd = lax.rem(k, 2)
        z = lax.rem(me_z + 4 + odd * ((k + 1) // 2) - (1 - odd) * (k // 2), 8)
        return z

    def gate(half, z, own=False):
        source = half * 8 + z
        block = stage.at[3, pl.ds(0, HEAD), :]
        pltpu.make_async_copy(block, block, own_sem.at[3] if own else grad_sem.at[source]).wait()
        at = pl.multiple_of(source * CONV, CONV)
        rows = pl.ds(at, CONV)
        grad = g_t[:, rows].T.astype(F32)
        grad_nat[rows, :] = grad
        gated = (grad * slope[rows, :]).astype(BF16).astype(F32)
        pre[pl.ds(pl.multiple_of(PAD + at, PAD), CONV), :] = gated

    def conv_back(step, _):
        at = pl.multiple_of(step * CONV, CONV)
        rows = pl.ds(at, CONV)
        parts = shifts(pre, at)
        total = grad_nat[rows, :].reshape(CONV // 8, 8, WIDE)
        for offset in by_shift:
            total = total + weights[KERNEL - offset][None] * moved(parts, offset)
        total = total.reshape(CONV, WIDE)
        place = at + lax.broadcasted_iota(jnp.int32, (CONV, WIDE), 0)
        lane = lax.broadcasted_iota(jnp.int32, (CONV, WIDE), 1)
        total = jnp.where((place < length) & (lane < HEAD), total, 0.0).astype(BF16).astype(F32)
        scaled = (total * upper[rows, :]).astype(BF16).astype(F32)
        delta = -jnp.sum(scaled * out_nat[rows, :], axis=1, keepdims=True)
        high = delta.astype(BF16).astype(F32)
        middle = (delta - high).astype(BF16).astype(F32)
        last = delta - high - middle
        scaled = jnp.where(lane == HEAD, high, scaled)
        scaled = jnp.where(lane == HEAD + 1, middle, scaled)
        scaled = jnp.where(lane == HEAD + 2, last, scaled).astype(BF16)
        grad_x[rows, :] = scaled
        grad_t[:, rows] = scaled.T
        return 0

    def gate_both(k, _):
        gate(1 - me_y, rank(k))
        gate(me_y, rank(k))
        return 0

    def back_both(k, _):
        for half in (0, 1):
            conv_back(half * 8 + rank(k), 0)
        return 0

    def gate_and_back(k, _):
        gate_both(k, 0)
        return back_both(k - 2, 0)

    lax.fori_loop(0, 2, gate_both, 0)
    lax.fori_loop(2, 7, gate_and_back, 0)
    gate(1 - me_y, me_z)
    gate(me_y, me_z, own=True)
    lax.fori_loop(5, 8, back_both, 0)

    out_sent = [len(landings) + i for i in range(3)]

    def send_back(which, step):
        for part in range(ROWS // frames):
            peer = step * (ROWS // frames) + part
            source = stage_out.at[which, pl.ds(pl.multiple_of(peer * HEAD, HEAD), HEAD), :]
            target = back.at[which, own_rows, :]

            @pl.when(peer != me)
            def _():
                pltpu.make_async_remote_copy(
                    src_ref=source,
                    dst_ref=target,
                    send_sem=send_sem.at[out_sent[which]],
                    recv_sem=recv_sem.at[out_sent[which]],
                    device_id={"seq": peer},
                    device_id_type=MESH,
                ).start()

    def put(which, step, block):
        for part in range(ROWS // frames):
            peer = step * (ROWS // frames) + part
            piece = block[:, part * frames : (part + 1) * frames]
            stage_out[which, pl.ds(pl.multiple_of(peer * HEAD, HEAD), HEAD), :] = piece
        send_back(which, step)


    def far_first(step):
        k = step // 2
        odd = lax.rem(k, 2)
        pair = lax.rem(me_z // 2 + 2 + (1 - odd) * (k // 2) - odd * ((k + 1) // 2) + 4, 4)
        return lax.rem(me_y + 1 + lax.rem(step, 2), 2) * 4 + pair

    def value_step(step, _):
        step = far_first(step)
        columns = pl.ds(pl.multiple_of(step * ROWS, ROWS), ROWS)
        block = jnp.dot(grad_t[0:HEAD, :], low[:, columns], preferred_element_type=F32)
        put(2, step, block.astype(BF16))
        return 0

    lax.fori_loop(0, steps, value_step, 0)

    def taps(step, _):
        at = pl.multiple_of(step * CONV, CONV)
        parts = shifts(att, at)
        gated = pre[pl.ds(pl.multiple_of(PAD + at, PAD), CONV), :].reshape(CONV // 8, 8, WIDE)
        for offset in by_shift:
            tap_sum[offset - 1] += jnp.sum(gated * moved(parts, offset), axis=0)
        tap_sum[KERNEL] += jnp.sum(gated, axis=0)
        return 0

    lax.fori_loop(0, seq_len // CONV, taps, 0)

    def sum_start(level, slots, mine, peers, value):
        slots[mine] = value
        for peer in peers:
            pltpu.make_async_remote_copy(
                src_ref=slots.at[mine],
                dst_ref=slots.at[mine],
                send_sem=sum_send.at[level],
                recv_sem=sum_recv.at[level],
                device_id={"dp": peer},
                device_id_type=MESH,
            ).start()

    def sum_end(level, slots, peers):
        whole = slots.at[pl.ds(0, len(peers))]
        pltpu.make_async_copy(whole, whole, sum_recv.at[level]).wait()
        value = slots[0]
        for i in range(1, len(peers) + 1):
            value = value + slots[i]
        return value

    sum_start(0, one, dp_core, core_peers, jnp.sum(tap_sum[...], axis=1))

    back_scale = F32(1.0 / math.sqrt(HEAD))

    def query_step(step, _):
        step = far_first(step)
        rows = pl.ds(pl.multiple_of(step * ROWS, ROWS), ROWS)
        change = jnp.dot(grad_x[rows, :], v_t[...], preferred_element_type=F32)
        diff = (change * low[rows, :].astype(F32)).astype(BF16)
        low[rows, :] = diff
        block = jnp.dot(diff, k_nat[...], preferred_element_type=F32)
        put(0, step, (block * back_scale).astype(BF16).T[0:HEAD, :])
        return 0

    lax.fori_loop(0, steps, query_step, 0)
    sum_start(1, two, dp_x, x_peers, sum_end(0, one, core_peers))

    def key_step(step, _):
        step = far_first(step)
        columns = pl.ds(pl.multiple_of(step * ROWS, ROWS), ROWS)
        block = jnp.dot(q_t[0:HEAD, :], low[:, columns], preferred_element_type=F32)
        put(1, step, (block * back_scale).astype(BF16))
        return 0

    lax.fori_loop(0, steps, key_step, 0)
    sum_start(2, three, dp_y, y_peers, sum_end(1, two, x_peers))
    sums = sum_end(2, three, y_peers)
    dw_ref[...] = sums[0:KERNEL, 0:HEAD]
    db_ref[...] = sums[KERNEL : KERNEL + 1, 0:HEAD]

    stores = []
    for which, result in ((2, dv_ref), (0, dq_ref), (1, dk_ref)):
        back[which, own_rows, :] = stage_out[which, own_rows, :]
        whole = back.at[which, others, :]
        pltpu.make_async_copy(whole, whole, recv_sem.at[out_sent[which]]).wait()
        for b in range(width // WIDE):
            done[which, :, b * WIDE : (b + 1) * WIDE] = back[which, b * WIDE : (b + 1) * WIDE, :].T
        store = pltpu.make_async_copy(done.at[which], result.at[0], store_sem.at[which])
        store.start()
        stores.append(store)
    for store in stores:
        store.wait()
    for i in range(1 if early else 0, len(landings) + 3):
        sent(i)
    for level, (slots, peers) in enumerate(((one, core_peers), (two, x_peers), (three, y_peers))):
        whole = slots.at[pl.ds(0, len(peers))]
        pltpu.make_async_copy(whole, whole, sum_send.at[level]).wait()


def hand_over(*refs):
    sems = refs[-1]
    copies = [pltpu.make_async_copy(refs[i], refs[5 + i], sems.at[i]) for i in range(5)]
    for copy in copies:
        copy.start()
    for copy in copies:
        copy.wait()


def on_device(queries, keys, values, grad_out, conv_weight, conv_bias, lengths):
    _, frames, width = queries.shape
    seq_len = frames * HEADS
    any_spec = pl.BlockSpec(memory_space=pl.ANY)
    vmem = pl.BlockSpec(memory_space=pltpu.VMEM)
    block = jax.ShapeDtypeStruct(queries.shape, BF16)
    tall = seq_len + 2 * PAD
    query_grad, key_grad, value_grad, weight_grad, bias_grad = pl.pallas_call(
        core,
        out_shape=(
            block,
            block,
            block,
            jax.ShapeDtypeStruct((KERNEL, HEAD), F32),
            jax.ShapeDtypeStruct((1, HEAD), F32),
        ),
        in_specs=[any_spec] * 4 + [vmem, vmem, pl.BlockSpec(memory_space=pltpu.SMEM)],
        out_specs=(any_spec,) * 3 + (vmem,) * 2,
        scratch_shapes=[
            pltpu.VMEM((4, frames, width), BF16),
            pltpu.VMEM((4, width, frames), BF16),
            pltpu.VMEM((WIDE, seq_len), BF16),
            pltpu.VMEM((WIDE, seq_len), BF16),
            pltpu.VMEM((WIDE, seq_len), BF16),
            pltpu.VMEM((WIDE, seq_len), BF16),
            pltpu.VMEM((KERNEL + 1, 8, WIDE), F32),
            pltpu.VMEM((seq_len, seq_len), BF16),
            pltpu.VMEM((tall, WIDE), F32),
            pltpu.VMEM((seq_len, WIDE), F32),
            pltpu.VMEM((seq_len, WIDE), F32),
            pltpu.VMEM((tall, WIDE), F32),
            pltpu.VMEM((seq_len, WIDE), F32),
            pltpu.VMEM((seq_len, WIDE), BF16),
            pltpu.VMEM((WIDE, seq_len), BF16),
            pltpu.VMEM((seq_len, WIDE), F32),
            pltpu.VMEM((seq_len, WIDE), BF16),
            pltpu.VMEM((seq_len, WIDE), BF16),
            pltpu.VMEM((3, width, frames), BF16),
            pltpu.VMEM((3, width, frames), BF16),
            pltpu.VMEM((3, frames, width), BF16),
            pltpu.VMEM((KERNEL + 1, 8, WIDE), F32),
            pltpu.VMEM((2, KERNEL + 1, WIDE), F32),
            pltpu.VMEM((4, KERNEL + 1, WIDE), F32),
            pltpu.VMEM((4, KERNEL + 1, WIDE), F32),
            pltpu.SemaphoreType.DMA((4,)),
            pltpu.SemaphoreType.DMA((4,)),
            pltpu.SemaphoreType.DMA((7,)),
            pltpu.SemaphoreType.DMA((7,)),
            pltpu.SemaphoreType.DMA((HEADS,)),
            pltpu.SemaphoreType.DMA((3,)),
            pltpu.SemaphoreType.DMA((3,)),
            pltpu.SemaphoreType.DMA((3,)),
        ],
        compiler_params=pltpu.CompilerParams(
            collective_id=0, has_side_effects=True, vmem_limit_bytes=56 << 20
        ),
    )(queries, keys, values, grad_out, conv_weight, conv_bias, lengths)
    found = (query_grad, key_grad, value_grad, weight_grad, bias_grad)
    found = pl.pallas_call(
        hand_over,
        out_shape=tuple(jax.ShapeDtypeStruct(part.shape, part.dtype) for part in found),
        in_specs=[vmem] * 5,
        out_specs=(any_spec,) * 5,
        scratch_shapes=[pltpu.SemaphoreType.DMA((5,))],
    )(*found)
    return *found[:4], found[4][0]


def solution(mesh):
    return jax.shard_map(
        on_device,
        mesh=mesh,
        in_specs=(
            P("dp", "seq", None),
            P("dp", "seq", None),
            P("dp", "seq", None),
            P("dp", "seq", None),
            P(),
            P(),
            P("dp"),
        ),
        out_specs=(
            P("dp", "seq", None),
            P("dp", "seq", None),
            P("dp", "seq", None),
            P(None, "seq"),
            P("seq"),
        ),
        check_vma=False,
    )
```

```python
import math

import jax
import jax.numpy as jnp
from jax import lax
from jax.experimental import pallas as pl
from jax.experimental.pallas import tpu as pltpu
from jax.sharding import PartitionSpec as P

MESH = pl.DeviceIdType.MESH
HEADS = 16
KERNEL = 31
EARLY = False
HEAD = 96
WIDE = 128
PAD = 16
ROWS = 256
CONV = 128
NEG = -1e30
F32 = jnp.float32
BF16 = jnp.bfloat16


def core(
    q_hbm, k_hbm, v_hbm, g_hbm, weight_ref, bias_ref, length_ref,
    dq_ref, dk_ref, dv_ref, dw_ref, db_ref,
    raw, stage, q_t, k_t, v_t, g_t, weights, low, att, out_nat, slope, pre, upper,
    grad_x, grad_t, grad_nat, k_nat, diffs, stage_out, back, done, tap_sum, one, two, three,
    load_sem, own_sem, send_sem, recv_sem, block_sem, store_sem, sum_send, sum_recv,
):
    seq_len = q_t.shape[1]
    frames = raw.shape[1]
    width = raw.shape[2]
    me = lax.axis_index("seq")
    dp = lax.axis_index("dp")
    dp_core = lax.rem(dp, 2)
    dp_x = lax.rem(dp // 2, 4)
    dp_y = dp // 8
    length = length_ref[0]

    me_y, me_z = me // 8, lax.rem(me, 8)
    turns = [(dy, dz) for dz in (4, 3, 5, 2, 6, 1, 7, 0) for dy in (1, 0)][:-1]
    seq_peers = [lax.rem(me_y + dy, 2) * 8 + lax.rem(me_z + dz, 8) for dy, dz in turns]
    core_peers = [dp_y * 8 + dp_x * 2 + 1 - dp_core]
    x_peers = [dp_y * 8 + lax.rem(dp_x + s, 4) * 2 + dp_core for s in (1, 2, 3)]
    y_peers = [lax.rem(dp_y + s, 4) * 8 + dp_x * 2 + dp_core for s in (1, 2, 3)]
    barrier = pltpu.get_barrier_semaphore()
    for peer in seq_peers:
        pl.semaphore_signal(barrier, inc=1, device_id={"seq": peer}, device_id_type=MESH)
    for peer in core_peers + x_peers + y_peers:
        pl.semaphore_signal(barrier, inc=1, device_id={"dp": peer}, device_id_type=MESH)

    sources = (k_hbm, q_hbm, v_hbm, g_hbm)
    quarter = width // 4
    loads = {}
    for i, ref in enumerate(sources):
        for c in range(4):
            part = pl.ds(c * quarter, quarter)
            loads[i, c] = pltpu.make_async_copy(
                ref.at[0, :, part], raw.at[i, :, part], load_sem.at[i, c]
            )
            loads[i, c].start()

    own_lanes = pl.ds(pl.multiple_of(me * frames, frames), frames)
    own_rows = pl.ds(pl.multiple_of(me * HEAD, HEAD), HEAD)
    landings = (k_t, q_t, v_t, g_t)
    others = pl.ds(0, (HEADS - 1) * HEAD)

    early = EARLY

    def turn_around(i):
        for b in range(width // WIDE):
            if b * WIDE % quarter == 0:
                loads[i, b * WIDE // quarter].wait()
            stage[i, b * WIDE : (b + 1) * WIDE, :] = raw[i, :, b * WIDE : (b + 1) * WIDE].T

    def send(i):
        target = landings[i].at[pl.ds(0, HEAD), own_lanes]
        for peer in seq_peers:
            pltpu.make_async_remote_copy(
                src_ref=stage.at[i, pl.ds(pl.multiple_of(peer * HEAD, HEAD), HEAD), :],
                dst_ref=target,
                send_sem=send_sem.at[i],
                recv_sem=block_sem.at[i - 1, me] if i else recv_sem.at[i],
                device_id={"seq": peer},
                device_id_type=MESH,
            ).start()
        pltpu.make_async_copy(stage.at[i, own_rows, :], target, own_sem.at[i]).start()

    def sent(i):
        whole = stage.at[0, others, :]
        pltpu.make_async_copy(whole, whole, send_sem.at[i]).wait()

    def rank(k):
        odd = lax.rem(k, 2)
        z = lax.rem(me_z + 4 + odd * ((k + 1) // 2) - (1 - odd) * (k // 2), 8)
        return z

    def spots_of(k):
        return [half * 8 + rank(k) for half in (1 - me_y, me_y)]

    def rows_of(spots):
        return [pl.ds(pl.multiple_of(spot * CONV, CONV), CONV) for spot in spots]

    def landed(i, spot, own=False):
        block = stage.at[i, pl.ds(0, HEAD), :]
        sem = own_sem.at[i] if own else block_sem.at[i - 1, spot]
        pltpu.make_async_copy(block, block, sem).wait()

    def landed_pair(i, k, own):
        spots = spots_of(k)
        landed(i, spots[0])
        landed(i, spots[1], own)
        return rows_of(spots)

    def arrived(i):
        mine = stage.at[i, own_rows, :]
        pltpu.make_async_copy(mine, mine, own_sem.at[i]).wait()
        whole = landings[i].at[pl.ds(0, HEAD), pl.ds(0, seq_len - frames)]
        pltpu.make_async_copy(whole, whole, recv_sem.at[i]).wait()

    turn_around(0)
    turn_around(1)
    pl.semaphore_wait(barrier, len(seq_peers + core_peers + x_peers + y_peers))
    send(0)
    send(1)
    turn_around(2)
    send(2)
    turn_around(3)
    if not early:
        send(3)

    k_t[HEAD:, :] = jnp.zeros((WIDE - HEAD, seq_len), BF16)
    key_pos = lax.broadcasted_iota(jnp.int32, (16, seq_len), 1)
    key_row = lax.broadcasted_iota(jnp.int32, (16, seq_len), 0)
    mask = jnp.where((key_row == 0) & (key_pos >= length), F32(NEG), F32(0.0))
    k_t[HEAD : HEAD + 16, :] = mask.astype(BF16)
    q_t[HEAD:, :] = jnp.zeros((WIDE - HEAD, seq_len), BF16)
    q_t[HEAD : HEAD + 16, :] = jnp.where(key_row == 0, F32(1.0), F32(0.0)).astype(BF16)
    v_t[HEAD:, :] = jnp.zeros((WIDE - HEAD, seq_len), BF16)
    v_t[HEAD : HEAD + 16, :] = jnp.where(key_row < 3, F32(1.0), F32(0.0)).astype(BF16)
    g_t[HEAD:, :] = jnp.zeros((WIDE - HEAD, seq_len), BF16)
    first = pl.multiple_of((me * HEAD) // WIDE * WIDE, WIDE)
    second = pl.multiple_of(jnp.minimum((me * HEAD) // WIDE + 1, width // WIDE - 1) * WIDE, WIDE)

    def own_columns(ref):
        pair = [ref[..., pl.ds(first, WIDE)], ref[..., pl.ds(second, WIDE)]]
        both = jnp.concatenate([part.reshape(-1, WIDE) for part in pair], axis=1)
        part = both[:, 0:HEAD]
        for turn in range(1, 4):
            at = turn * HEAD % WIDE
            part = jnp.where(lax.rem(me, 4) == turn, both[:, at : at + HEAD], part)
        return part

    weights[...] = jnp.zeros(weights.shape, F32)
    own_taps = own_columns(weight_ref)
    for j in range(KERNEL):
        weights[j, :, 0:HEAD] = jnp.broadcast_to(own_taps[j : j + 1, :], (8, HEAD))
    weights[KERNEL, :, 0:HEAD] = jnp.broadcast_to(own_columns(bias_ref), (8, HEAD))
    zero_rim = jnp.zeros((PAD, WIDE), F32)
    for buffer in (att, pre):
        buffer[0:PAD, :] = zero_rim
        buffer[PAD + seq_len :, :] = zero_rim
    tap_sum[...] = jnp.zeros(tap_sum.shape, F32)
    out_nat[...] = jnp.zeros(out_nat.shape, F32)

    if early:
        sent(0)
        send(3)
    def turn(wide_ref, tall_ref):
        for b in range(seq_len // WIDE):
            part = slice(b * WIDE, (b + 1) * WIDE)
            tall_ref[part, :] = wide_ref[:, part].T

    arrived(0)
    turn(k_t, k_nat)

    rate = F32(math.log2(math.e) / math.sqrt(HEAD))
    steps = seq_len // ROWS

    def weigh(k, _, own=False):
        rows = landed_pair(1, k, own)
        query = jnp.concatenate([q_t[:, part] for part in rows], axis=1).T
        scores = jnp.dot(query, k_t[...], preferred_element_type=F32)
        top = jnp.max(scores, axis=1, keepdims=True)
        exped = jnp.exp2((scores - top) * rate).astype(BF16)
        for i in range(2):
            low[rows[i], :] = exped[i * CONV : (i + 1) * CONV, :]
        return 0

    def attend(k, _, own=False):
        rows = landed_pair(2, k, own)
        value = jnp.concatenate([v_t[:, part] for part in rows], axis=1).T
        exped = jnp.concatenate([low[:, part] for part in rows], axis=1)
        out_nat[...] += jnp.dot(exped, value, preferred_element_type=F32)
        return 0

    def forward(step, _):
        at = pl.multiple_of(step * ROWS, ROWS)
        rows = pl.ds(at, ROWS)
        out = out_nat[rows, :]
        inverse = 1.0 / out[:, HEAD : HEAD + 1]
        upper[rows, :] = jnp.broadcast_to(inverse, (ROWS, WIDE))
        out = out * inverse
        out_nat[rows, :] = out
        place = at + lax.broadcasted_iota(jnp.int32, (ROWS, WIDE), 0)
        lane = lax.broadcasted_iota(jnp.int32, (ROWS, WIDE), 1)
        shown = jnp.where((place < length) & (lane < HEAD), out, 0.0)
        att[pl.ds(pl.multiple_of(PAD + at, PAD), ROWS), :] = shown.astype(BF16).astype(F32)
        return 0

    def shifts(buffer, at):
        window = buffer[pl.ds(at, CONV + 2 * PAD), :]
        return [window[r : r + CONV + 2 * PAD - 8, :] for r in range(8)]

    def moved(parts, offset):
        aligned = offset // 8 * 8
        part = parts[offset % 8][aligned : aligned + CONV, :]
        return part.reshape(CONV // 8, 8, WIDE)

    lax.fori_loop(0, 7, weigh, 0)
    weigh(7, 0, own=True)
    lax.fori_loop(0, 7, attend, 0)
    attend(7, 0, own=True)
    by_shift = sorted(range(1, KERNEL + 1), key=lambda offset: offset % 8)

    def conv(step, _):
        at = pl.multiple_of(step * CONV, CONV)
        parts = shifts(att, at)
        total = jnp.broadcast_to(weights[KERNEL][None], (CONV // 8, 8, WIDE))
        for offset in by_shift:
            total = total + weights[offset - 1][None] * moved(parts, offset)
        total = total.reshape(CONV, WIDE)
        sig = jax.nn.sigmoid(total)
        slope[pl.ds(at, CONV), :] = sig * (1.0 + total * (1.0 - sig))
        return 0

    def conv_and_forward(step, _):
        conv(2 * step - 3, 0)
        conv(2 * step - 2, 0)
        return forward(step, 0)

    forward(0, 0)
    conv(0, 0)
    forward(1, 0)
    lax.fori_loop(2, steps, conv_and_forward, 0)
    lax.fori_loop(2 * steps - 3, 2 * steps, conv, 0)

    def gate(half, z, own=False):
        source = half * 8 + z
        landed(3, source, own)
        at = pl.multiple_of(source * CONV, CONV)
        rows = pl.ds(at, CONV)
        grad = g_t[:, rows].T.astype(F32)
        grad_nat[rows, :] = grad
        gated = (grad * slope[rows, :]).astype(BF16).astype(F32)
        pre[pl.ds(pl.multiple_of(PAD + at, PAD), CONV), :] = gated

    def conv_back(step, _):
        at = pl.multiple_of(step * CONV, CONV)
        rows = pl.ds(at, CONV)
        parts = shifts(pre, at)
        total = grad_nat[rows, :].reshape(CONV // 8, 8, WIDE)
        for offset in by_shift:
            total = total + weights[KERNEL - offset][None] * moved(parts, offset)
        total = total.reshape(CONV, WIDE)
        place = at + lax.broadcasted_iota(jnp.int32, (CONV, WIDE), 0)
        lane = lax.broadcasted_iota(jnp.int32, (CONV, WIDE), 1)
        total = jnp.where((place < length) & (lane < HEAD), total, 0.0).astype(BF16).astype(F32)
        scaled = (total * upper[rows, :]).astype(BF16).astype(F32)
        delta = -jnp.sum(scaled * out_nat[rows, :], axis=1, keepdims=True)
        high = delta.astype(BF16).astype(F32)
        middle = (delta - high).astype(BF16).astype(F32)
        last = delta - high - middle
        scaled = jnp.where(lane == HEAD, high, scaled)
        scaled = jnp.where(lane == HEAD + 1, middle, scaled)
        scaled = jnp.where(lane == HEAD + 2, last, scaled).astype(BF16)
        grad_x[rows, :] = scaled
        grad_t[:, rows] = scaled.T
        return 0

    out_sent = [len(landings) + i for i in range(3)]

    def send_one(which, peer):
        pltpu.make_async_remote_copy(
            src_ref=stage_out.at[which, pl.ds(pl.multiple_of(peer * HEAD, HEAD), HEAD), :],
            dst_ref=back.at[which, own_rows, :],
            send_sem=send_sem.at[out_sent[which]],
            recv_sem=recv_sem.at[out_sent[which]],
            device_id={"seq": peer},
            device_id_type=MESH,
        ).start()

    back_scale = F32(1.0 / math.sqrt(HEAD))

    def query_both(k):
        spots = spots_of(k)
        rows = rows_of(spots)
        grads = jnp.concatenate([grad_x[part, :] for part in rows], axis=0)
        change = jnp.dot(grads, v_t[...], preferred_element_type=F32)
        exped = jnp.concatenate([low[part, :] for part in rows], axis=0).astype(F32)
        diff = (change * exped).astype(BF16)
        block = jnp.dot(diff, k_nat[...], preferred_element_type=F32)
        block = (block * back_scale).astype(BF16).T[0:HEAD, :]
        for i in range(2):
            diffs[rows[i], :] = diff[i * CONV : (i + 1) * CONV, :]
            place = pl.ds(pl.multiple_of(spots[i] * HEAD, HEAD), HEAD)
            stage_out[0, place, :] = block[:, i * CONV : (i + 1) * CONV]
        return spots

    def gate_both(k, _):
        gate(1 - me_y, rank(k))
        gate(me_y, rank(k))
        return 0

    def back_both(k):
        for half in (1 - me_y, me_y):
            conv_back(half * 8 + rank(k), 0)

    def flow(k, _):
        gate_both(k, 0)
        for spot in query_and_back(k):
            send_one(0, spot)
        return 0

    def query_and_back(k):
        spots = query_both(k - 3)
        back_both(k - 2)
        return spots

    def flow_end(k, _):
        for spot in query_and_back(k):
            send_one(0, spot)
        return 0

    lax.fori_loop(0, 3, gate_both, 0)
    back_both(0)
    lax.fori_loop(3, 7, flow, 0)
    gate(1 - me_y, me_z)
    gate(me_y, me_z, own=True)
    lax.fori_loop(7, 10, flow_end, 0)
    send_one(0, query_both(7)[0])

    def send_back(which, step):
        for part in range(ROWS // frames):
            peer = step * (ROWS // frames) + part

            @pl.when(peer != me)
            def _():
                send_one(which, peer)

    def put(which, step, block):
        for part in range(ROWS // frames):
            peer = step * (ROWS // frames) + part
            piece = block[:, part * frames : (part + 1) * frames]
            stage_out[which, pl.ds(pl.multiple_of(peer * HEAD, HEAD), HEAD), :] = piece
        send_back(which, step)


    def far_first(step):
        k = step // 2
        odd = lax.rem(k, 2)
        pair = lax.rem(me_z // 2 + 2 + (1 - odd) * (k // 2) - odd * ((k + 1) // 2) + 4, 4)
        return lax.rem(me_y + 1 + lax.rem(step, 2), 2) * 4 + pair

    def value_step(step, _):
        step = far_first(step)
        columns = pl.ds(pl.multiple_of(step * ROWS, ROWS), ROWS)
        block = jnp.dot(grad_t[0:HEAD, :], low[:, columns], preferred_element_type=F32)
        put(2, step, block.astype(BF16))
        return 0

    lax.fori_loop(0, steps, value_step, 0)

    def taps(step, _):
        at = pl.multiple_of(step * CONV, CONV)
        parts = shifts(att, at)
        gated = pre[pl.ds(pl.multiple_of(PAD + at, PAD), CONV), :].reshape(CONV // 8, 8, WIDE)
        for offset in by_shift:
            tap_sum[offset - 1] += jnp.sum(gated * moved(parts, offset), axis=0)
        tap_sum[KERNEL] += jnp.sum(gated, axis=0)
        return 0

    lax.fori_loop(0, seq_len // CONV, taps, 0)

    def sum_start(level, slots, mine, peers, value):
        slots[mine] = value
        for peer in peers:
            pltpu.make_async_remote_copy(
                src_ref=slots.at[mine],
                dst_ref=slots.at[mine],
                send_sem=sum_send.at[level],
                recv_sem=sum_recv.at[level],
                device_id={"dp": peer},
                device_id_type=MESH,
            ).start()

    def sum_end(level, slots, peers):
        whole = slots.at[pl.ds(0, len(peers))]
        pltpu.make_async_copy(whole, whole, sum_recv.at[level]).wait()
        value = slots[0]
        for i in range(1, len(peers) + 1):
            value = value + slots[i]
        return value

    sum_start(0, one, dp_core, core_peers, jnp.sum(tap_sum[...], axis=1))


    def key_step(step, _):
        step = far_first(step)
        columns = pl.ds(pl.multiple_of(step * ROWS, ROWS), ROWS)
        block = jnp.dot(q_t[0:HEAD, :], diffs[:, columns], preferred_element_type=F32)
        put(1, step, (block * back_scale).astype(BF16))
        return 0

    lax.fori_loop(0, steps, key_step, 0)
    sum_start(1, two, dp_x, x_peers, sum_end(0, one, core_peers))

    stores = []

    def collect(which, result):
        back[which, own_rows, :] = stage_out[which, own_rows, :]
        whole = back.at[which, others, :]
        pltpu.make_async_copy(whole, whole, recv_sem.at[out_sent[which]]).wait()
        for b in range(width // WIDE):
            done[which, :, b * WIDE : (b + 1) * WIDE] = back[which, b * WIDE : (b + 1) * WIDE, :].T
            if (b + 1) * WIDE % quarter == 0:
                c = b * WIDE // quarter
                part = pl.ds(c * quarter, quarter)
                store = pltpu.make_async_copy(
                    done.at[which, :, part], result.at[0, :, part], store_sem.at[which, c]
                )
                store.start()
                stores.append(store)

    collect(0, dq_ref)
    sum_start(2, three, dp_y, y_peers, sum_end(1, two, x_peers))
    collect(2, dv_ref)
    sums = sum_end(2, three, y_peers)
    dw_ref[...] = sums[0:KERNEL, 0:HEAD]
    db_ref[...] = sums[KERNEL : KERNEL + 1, 0:HEAD]
    collect(1, dk_ref)
    for store in stores:
        store.wait()
    for i in range(1 if early else 0, len(landings) + 3):
        sent(i)
    for level, (slots, peers) in enumerate(((one, core_peers), (two, x_peers), (three, y_peers))):
        whole = slots.at[pl.ds(0, len(peers))]
        pltpu.make_async_copy(whole, whole, sum_send.at[level]).wait()


def hand_over(*refs):
    given, results, held, small, bias, in_sem, out_sem = refs[:5], refs[5:10], *refs[10:]
    quarter = held.shape[2] // 4
    copies = []
    for i in range(3):
        for c in range(4):
            part = pl.ds(c * quarter, quarter)
            where = held.at[i, :, part]
            copies.append(
                (
                    pltpu.make_async_copy(given[i].at[0, :, part], where, in_sem.at[4 * i + c]),
                    pltpu.make_async_copy(where, results[i].at[0, :, part], out_sem.at[4 * i + c]),
                )
            )
    for i, where in ((3, small), (4, bias)):
        copies.append(
            (
                pltpu.make_async_copy(given[i], where, in_sem.at[9 + i]),
                pltpu.make_async_copy(where, results[i], out_sem.at[9 + i]),
            )
        )
    for fetch, _ in copies:
        fetch.start()
    for fetch, put in copies:
        fetch.wait()
        put.start()
    for _, put in copies:
        put.wait()


def on_device(queries, keys, values, grad_out, conv_weight, conv_bias, lengths):
    _, frames, width = queries.shape
    seq_len = frames * HEADS
    any_spec = pl.BlockSpec(memory_space=pl.ANY)
    vmem = pl.BlockSpec(memory_space=pltpu.VMEM)
    block = jax.ShapeDtypeStruct(queries.shape, BF16)
    tall = seq_len + 2 * PAD
    query_grad, key_grad, value_grad, weight_grad, bias_grad = pl.pallas_call(
        core,
        out_shape=(
            block,
            block,
            block,
            jax.ShapeDtypeStruct((KERNEL, HEAD), F32),
            jax.ShapeDtypeStruct((1, HEAD), F32),
        ),
        in_specs=[any_spec] * 4 + [vmem, vmem, pl.BlockSpec(memory_space=pltpu.SMEM)],
        out_specs=(any_spec,) * 3 + (vmem,) * 2,
        scratch_shapes=[
            pltpu.VMEM((4, frames, width), BF16),
            pltpu.VMEM((4, width, frames), BF16),
            pltpu.VMEM((WIDE, seq_len), BF16),
            pltpu.VMEM((WIDE, seq_len), BF16),
            pltpu.VMEM((WIDE, seq_len), BF16),
            pltpu.VMEM((WIDE, seq_len), BF16),
            pltpu.VMEM((KERNEL + 1, 8, WIDE), F32),
            pltpu.VMEM((seq_len, seq_len), BF16),
            pltpu.VMEM((tall, WIDE), F32),
            pltpu.VMEM((seq_len, WIDE), F32),
            pltpu.VMEM((seq_len, WIDE), F32),
            pltpu.VMEM((tall, WIDE), F32),
            pltpu.VMEM((seq_len, WIDE), F32),
            pltpu.VMEM((seq_len, WIDE), BF16),
            pltpu.VMEM((WIDE, seq_len), BF16),
            pltpu.VMEM((seq_len, WIDE), F32),
            pltpu.VMEM((seq_len, WIDE), BF16),
            pltpu.VMEM((seq_len, seq_len), BF16),
            pltpu.VMEM((3, width, frames), BF16),
            pltpu.VMEM((3, width, frames), BF16),
            pltpu.VMEM((3, frames, width), BF16),
            pltpu.VMEM((KERNEL + 1, 8, WIDE), F32),
            pltpu.VMEM((2, KERNEL + 1, WIDE), F32),
            pltpu.VMEM((4, KERNEL + 1, WIDE), F32),
            pltpu.VMEM((4, KERNEL + 1, WIDE), F32),
            pltpu.SemaphoreType.DMA((4, 4)),
            pltpu.SemaphoreType.DMA((4,)),
            pltpu.SemaphoreType.DMA((7,)),
            pltpu.SemaphoreType.DMA((7,)),
            pltpu.SemaphoreType.DMA((3, HEADS)),
            pltpu.SemaphoreType.DMA((3, 4)),
            pltpu.SemaphoreType.DMA((3,)),
            pltpu.SemaphoreType.DMA((3,)),
        ],
        compiler_params=pltpu.CompilerParams(
            collective_id=0, has_side_effects=True, vmem_limit_bytes=56 << 20
        ),
    )(queries, keys, values, grad_out, conv_weight, conv_bias, lengths)
    found = (query_grad, key_grad, value_grad, weight_grad, bias_grad)
    found = pl.pallas_call(
        hand_over,
        out_shape=tuple(jax.ShapeDtypeStruct(part.shape, part.dtype) for part in found),
        in_specs=[any_spec] * 5,
        out_specs=(any_spec,) * 5,
        scratch_shapes=[
            pltpu.VMEM((3, frames, width), BF16),
            pltpu.VMEM((KERNEL, HEAD), F32),
            pltpu.VMEM((1, HEAD), F32),
            pltpu.SemaphoreType.DMA((14,)),
            pltpu.SemaphoreType.DMA((14,)),
        ],
        compiler_params=pltpu.CompilerParams(vmem_limit_bytes=56 << 20),
    )(*found)
    return *found[:4], found[4][0]


def solution(mesh):
    return jax.shard_map(
        on_device,
        mesh=mesh,
        in_specs=(
            P("dp", "seq", None),
            P("dp", "seq", None),
            P("dp", "seq", None),
            P("dp", "seq", None),
            P(),
            P(),
            P("dp"),
        ),
        out_specs=(
            P("dp", "seq", None),
            P("dp", "seq", None),
            P("dp", "seq", None),
            P(None, "seq"),
            P("seq"),
        ),
        check_vma=False,
    )
```

```python
import math

import jax
import jax.numpy as jnp
from jax import lax
from jax.experimental import pallas as pl
from jax.experimental.pallas import tpu as pltpu
from jax.sharding import PartitionSpec as P

MESH = pl.DeviceIdType.MESH
HEADS = 16
KERNEL = 31
EARLY = False
HEAD = 96
WIDE = 128
PAD = 16
ROWS = 256
CONV = 128
NEG = -1e30
F32 = jnp.float32
BF16 = jnp.bfloat16


def core(
    q_hbm, k_hbm, v_hbm, g_hbm, weight_ref, bias_ref, length_ref,
    dq_ref, dk_ref, dv_ref, dw_ref, db_ref,
    raw, stage, q_t, k_t, v_t, g_t, weights, low, att, out_nat, slope, pre, upper,
    grad_x, grad_t, grad_nat, k_nat, diffs, stage_out, back, tap_sum, one, two, three,
    load_sem, own_sem, send_sem, recv_sem, block_sem, sum_send, sum_recv,
):
    seq_len = q_t.shape[1]
    frames = raw.shape[1]
    width = raw.shape[2]
    me = lax.axis_index("seq")
    dp = lax.axis_index("dp")
    dp_core = lax.rem(dp, 2)
    dp_x = lax.rem(dp // 2, 4)
    dp_y = dp // 8
    length = length_ref[0]

    me_y, me_z = me // 8, lax.rem(me, 8)
    turns = [(dy, dz) for dz in (4, 3, 5, 2, 6, 1, 7, 0) for dy in (1, 0)][:-1]
    seq_peers = [lax.rem(me_y + dy, 2) * 8 + lax.rem(me_z + dz, 8) for dy, dz in turns]
    core_peers = [dp_y * 8 + dp_x * 2 + 1 - dp_core]
    x_peers = [dp_y * 8 + lax.rem(dp_x + s, 4) * 2 + dp_core for s in (1, 2, 3)]
    y_peers = [lax.rem(dp_y + s, 4) * 8 + dp_x * 2 + dp_core for s in (1, 2, 3)]
    barrier = pltpu.get_barrier_semaphore()
    for peer in seq_peers:
        pl.semaphore_signal(barrier, inc=1, device_id={"seq": peer}, device_id_type=MESH)
    for peer in core_peers + x_peers + y_peers:
        pl.semaphore_signal(barrier, inc=1, device_id={"dp": peer}, device_id_type=MESH)

    sources = (k_hbm, q_hbm, v_hbm, g_hbm)
    quarter = width // 4
    loads = {}
    for i, ref in enumerate(sources):
        for c in range(4):
            part = pl.ds(c * quarter, quarter)
            loads[i, c] = pltpu.make_async_copy(
                ref.at[0, :, part], raw.at[i, :, part], load_sem.at[i, c]
            )
            loads[i, c].start()

    own_lanes = pl.ds(pl.multiple_of(me * frames, frames), frames)
    own_rows = pl.ds(pl.multiple_of(me * HEAD, HEAD), HEAD)
    landings = (k_t, q_t, v_t, g_t)
    others = pl.ds(0, (HEADS - 1) * HEAD)

    early = EARLY

    def turn_around(i):
        for b in range(width // WIDE):
            if b * WIDE % quarter == 0:
                loads[i, b * WIDE // quarter].wait()
            stage[i, b * WIDE : (b + 1) * WIDE, :] = raw[i, :, b * WIDE : (b + 1) * WIDE].T

    def send(i):
        target = landings[i].at[pl.ds(0, HEAD), own_lanes]
        for peer in seq_peers:
            pltpu.make_async_remote_copy(
                src_ref=stage.at[i, pl.ds(pl.multiple_of(peer * HEAD, HEAD), HEAD), :],
                dst_ref=target,
                send_sem=send_sem.at[i],
                recv_sem=block_sem.at[i - 1, me] if i else recv_sem.at[i],
                device_id={"seq": peer},
                device_id_type=MESH,
            ).start()
        pltpu.make_async_copy(stage.at[i, own_rows, :], target, own_sem.at[i]).start()

    def sent(i):
        whole = stage.at[0, others, :]
        pltpu.make_async_copy(whole, whole, send_sem.at[i]).wait()

    def rank(k):
        odd = lax.rem(k, 2)
        z = lax.rem(me_z + 4 + odd * ((k + 1) // 2) - (1 - odd) * (k // 2), 8)
        return z

    def spots_of(k):
        return [half * 8 + rank(k) for half in (1 - me_y, me_y)]

    def rows_of(spots):
        return [pl.ds(pl.multiple_of(spot * CONV, CONV), CONV) for spot in spots]

    def landed(i, spot, own=False):
        block = stage.at[i, pl.ds(0, HEAD), :]
        sem = own_sem.at[i] if own else block_sem.at[i - 1, spot]
        pltpu.make_async_copy(block, block, sem).wait()

    def landed_pair(i, k, own):
        spots = spots_of(k)
        landed(i, spots[0])
        landed(i, spots[1], own)
        return rows_of(spots)

    def arrived(i):
        mine = stage.at[i, own_rows, :]
        pltpu.make_async_copy(mine, mine, own_sem.at[i]).wait()
        whole = landings[i].at[pl.ds(0, HEAD), pl.ds(0, seq_len - frames)]
        pltpu.make_async_copy(whole, whole, recv_sem.at[i]).wait()

    turn_around(0)
    turn_around(1)
    pl.semaphore_wait(barrier, len(seq_peers + core_peers + x_peers + y_peers))
    send(0)
    send(1)
    turn_around(2)
    send(2)
    turn_around(3)
    if not early:
        send(3)

    k_t[HEAD:, :] = jnp.zeros((WIDE - HEAD, seq_len), BF16)
    key_pos = lax.broadcasted_iota(jnp.int32, (16, seq_len), 1)
    key_row = lax.broadcasted_iota(jnp.int32, (16, seq_len), 0)
    mask = jnp.where((key_row == 0) & (key_pos >= length), F32(NEG), F32(0.0))
    k_t[HEAD : HEAD + 16, :] = mask.astype(BF16)
    q_t[HEAD:, :] = jnp.zeros((WIDE - HEAD, seq_len), BF16)
    q_t[HEAD : HEAD + 16, :] = jnp.where(key_row == 0, F32(1.0), F32(0.0)).astype(BF16)
    v_t[HEAD:, :] = jnp.zeros((WIDE - HEAD, seq_len), BF16)
    v_t[HEAD : HEAD + 16, :] = jnp.where(key_row < 3, F32(1.0), F32(0.0)).astype(BF16)
    g_t[HEAD:, :] = jnp.zeros((WIDE - HEAD, seq_len), BF16)
    first = pl.multiple_of((me * HEAD) // WIDE * WIDE, WIDE)
    second = pl.multiple_of(jnp.minimum((me * HEAD) // WIDE + 1, width // WIDE - 1) * WIDE, WIDE)

    def own_columns(ref):
        pair = [ref[..., pl.ds(first, WIDE)], ref[..., pl.ds(second, WIDE)]]
        both = jnp.concatenate([part.reshape(-1, WIDE) for part in pair], axis=1)
        part = both[:, 0:HEAD]
        for turn in range(1, 4):
            at = turn * HEAD % WIDE
            part = jnp.where(lax.rem(me, 4) == turn, both[:, at : at + HEAD], part)
        return part

    weights[...] = jnp.zeros(weights.shape, F32)
    own_taps = own_columns(weight_ref)
    for j in range(KERNEL):
        weights[j, :, 0:HEAD] = jnp.broadcast_to(own_taps[j : j + 1, :], (8, HEAD))
    weights[KERNEL, :, 0:HEAD] = jnp.broadcast_to(own_columns(bias_ref), (8, HEAD))
    zero_rim = jnp.zeros((PAD, WIDE), F32)
    for buffer in (att, pre):
        buffer[0:PAD, :] = zero_rim
        buffer[PAD + seq_len :, :] = zero_rim
    tap_sum[...] = jnp.zeros(tap_sum.shape, F32)
    out_nat[...] = jnp.zeros(out_nat.shape, F32)

    if early:
        sent(0)
        send(3)
    def turn(wide_ref, tall_ref):
        for b in range(seq_len // WIDE):
            part = slice(b * WIDE, (b + 1) * WIDE)
            tall_ref[part, :] = wide_ref[:, part].T

    arrived(0)
    turn(k_t, k_nat)

    rate = F32(math.log2(math.e) / math.sqrt(HEAD))
    steps = seq_len // ROWS

    def weigh(k, _, own=False):
        rows = landed_pair(1, k, own)
        query = jnp.concatenate([q_t[:, part] for part in rows], axis=1).T
        scores = jnp.dot(query, k_t[...], preferred_element_type=F32)
        top = jnp.max(scores, axis=1, keepdims=True)
        exped = jnp.exp2((scores - top) * rate).astype(BF16)
        for i in range(2):
            low[rows[i], :] = exped[i * CONV : (i + 1) * CONV, :]
        return 0

    def attend(k, _, own=False):
        rows = landed_pair(2, k, own)
        value = jnp.concatenate([v_t[:, part] for part in rows], axis=1).T
        exped = jnp.concatenate([low[:, part] for part in rows], axis=1)
        out_nat[...] += jnp.dot(exped, value, preferred_element_type=F32)
        return 0

    def forward(step, _):
        at = pl.multiple_of(step * ROWS, ROWS)
        rows = pl.ds(at, ROWS)
        out = out_nat[rows, :]
        inverse = 1.0 / out[:, HEAD : HEAD + 1]
        upper[rows, :] = jnp.broadcast_to(inverse, (ROWS, WIDE))
        out = out * inverse
        out_nat[rows, :] = out
        place = at + lax.broadcasted_iota(jnp.int32, (ROWS, WIDE), 0)
        lane = lax.broadcasted_iota(jnp.int32, (ROWS, WIDE), 1)
        shown = jnp.where((place < length) & (lane < HEAD), out, 0.0)
        att[pl.ds(pl.multiple_of(PAD + at, PAD), ROWS), :] = shown.astype(BF16).astype(F32)
        return 0

    def shifts(buffer, at):
        window = buffer[pl.ds(at, CONV + 2 * PAD), :]
        return [window[r : r + CONV + 2 * PAD - 8, :] for r in range(8)]

    def moved(parts, offset):
        aligned = offset // 8 * 8
        part = parts[offset % 8][aligned : aligned + CONV, :]
        return part.reshape(CONV // 8, 8, WIDE)

    lax.fori_loop(0, 7, weigh, 0)
    weigh(7, 0, own=True)
    lax.fori_loop(0, 7, attend, 0)
    attend(7, 0, own=True)
    by_shift = sorted(range(1, KERNEL + 1), key=lambda offset: offset % 8)

    def conv(step, _):
        at = pl.multiple_of(step * CONV, CONV)
        parts = shifts(att, at)
        total = jnp.broadcast_to(weights[KERNEL][None], (CONV // 8, 8, WIDE))
        for offset in by_shift:
            total = total + weights[offset - 1][None] * moved(parts, offset)
        total = total.reshape(CONV, WIDE)
        sig = jax.nn.sigmoid(total)
        slope[pl.ds(at, CONV), :] = sig * (1.0 + total * (1.0 - sig))
        return 0

    def conv_and_forward(step, _):
        conv(2 * step - 3, 0)
        conv(2 * step - 2, 0)
        return forward(step, 0)

    forward(0, 0)
    conv(0, 0)
    forward(1, 0)
    lax.fori_loop(2, steps, conv_and_forward, 0)
    lax.fori_loop(2 * steps - 3, 2 * steps, conv, 0)

    def gate(half, z, own=False):
        source = half * 8 + z
        landed(3, source, own)
        at = pl.multiple_of(source * CONV, CONV)
        rows = pl.ds(at, CONV)
        grad = g_t[:, rows].T.astype(F32)
        grad_nat[rows, :] = grad
        gated = (grad * slope[rows, :]).astype(BF16).astype(F32)
        pre[pl.ds(pl.multiple_of(PAD + at, PAD), CONV), :] = gated

    def conv_back(step, _):
        at = pl.multiple_of(step * CONV, CONV)
        rows = pl.ds(at, CONV)
        parts = shifts(pre, at)
        total = grad_nat[rows, :].reshape(CONV // 8, 8, WIDE)
        for offset in by_shift:
            total = total + weights[KERNEL - offset][None] * moved(parts, offset)
        total = total.reshape(CONV, WIDE)
        place = at + lax.broadcasted_iota(jnp.int32, (CONV, WIDE), 0)
        lane = lax.broadcasted_iota(jnp.int32, (CONV, WIDE), 1)
        total = jnp.where((place < length) & (lane < HEAD), total, 0.0).astype(BF16).astype(F32)
        scaled = (total * upper[rows, :]).astype(BF16).astype(F32)
        delta = -jnp.sum(scaled * out_nat[rows, :], axis=1, keepdims=True)
        high = delta.astype(BF16).astype(F32)
        middle = (delta - high).astype(BF16).astype(F32)
        last = delta - high - middle
        scaled = jnp.where(lane == HEAD, high, scaled)
        scaled = jnp.where(lane == HEAD + 1, middle, scaled)
        scaled = jnp.where(lane == HEAD + 2, last, scaled).astype(BF16)
        grad_x[rows, :] = scaled
        grad_t[:, rows] = scaled.T
        return 0

    out_sent = [len(landings) + i for i in range(3)]

    def send_one(which, peer):
        pltpu.make_async_remote_copy(
            src_ref=stage_out.at[which, pl.ds(pl.multiple_of(peer * HEAD, HEAD), HEAD), :],
            dst_ref=back.at[which, own_rows, :],
            send_sem=send_sem.at[out_sent[which]],
            recv_sem=recv_sem.at[out_sent[which]],
            device_id={"seq": peer},
            device_id_type=MESH,
        ).start()

    back_scale = F32(1.0 / math.sqrt(HEAD))

    def query_both(k):
        spots = spots_of(k)
        rows = rows_of(spots)
        grads = jnp.concatenate([grad_x[part, :] for part in rows], axis=0)
        change = jnp.dot(grads, v_t[...], preferred_element_type=F32)
        exped = jnp.concatenate([low[part, :] for part in rows], axis=0).astype(F32)
        diff = (change * exped).astype(BF16)
        block = jnp.dot(diff, k_nat[...], preferred_element_type=F32)
        block = (block * back_scale).astype(BF16).T[0:HEAD, :]
        for i in range(2):
            diffs[rows[i], :] = diff[i * CONV : (i + 1) * CONV, :]
            place = pl.ds(pl.multiple_of(spots[i] * HEAD, HEAD), HEAD)
            stage_out[0, place, :] = block[:, i * CONV : (i + 1) * CONV]
        return spots

    def gate_both(k, _):
        gate(1 - me_y, rank(k))
        gate(me_y, rank(k))
        return 0

    def back_both(k):
        for half in (1 - me_y, me_y):
            conv_back(half * 8 + rank(k), 0)

    def flow(k, _):
        gate_both(k, 0)
        for spot in query_and_back(k):
            send_one(0, spot)
        return 0

    def query_and_back(k):
        spots = query_both(k - 3)
        back_both(k - 2)
        return spots

    def flow_end(k, _):
        for spot in query_and_back(k):
            send_one(0, spot)
        return 0

    lax.fori_loop(0, 3, gate_both, 0)
    back_both(0)
    lax.fori_loop(3, 7, flow, 0)
    gate(1 - me_y, me_z)
    gate(me_y, me_z, own=True)
    lax.fori_loop(7, 10, flow_end, 0)
    send_one(0, query_both(7)[0])

    def send_back(which, step):
        for part in range(ROWS // frames):
            peer = step * (ROWS // frames) + part

            @pl.when(peer != me)
            def _():
                send_one(which, peer)

    def put(which, step, block):
        for part in range(ROWS // frames):
            peer = step * (ROWS // frames) + part
            piece = block[:, part * frames : (part + 1) * frames]
            stage_out[which, pl.ds(pl.multiple_of(peer * HEAD, HEAD), HEAD), :] = piece
        send_back(which, step)


    def far_first(step):
        k = step // 2
        odd = lax.rem(k, 2)
        pair = lax.rem(me_z // 2 + 2 + (1 - odd) * (k // 2) - odd * ((k + 1) // 2) + 4, 4)
        return lax.rem(me_y + 1 + lax.rem(step, 2), 2) * 4 + pair

    def value_step(step, _):
        step = far_first(step)
        columns = pl.ds(pl.multiple_of(step * ROWS, ROWS), ROWS)
        block = jnp.dot(grad_t[0:HEAD, :], low[:, columns], preferred_element_type=F32)
        put(2, step, block.astype(BF16))
        return 0

    lax.fori_loop(0, steps, value_step, 0)

    def taps(step, _):
        at = pl.multiple_of(step * CONV, CONV)
        parts = shifts(att, at)
        gated = pre[pl.ds(pl.multiple_of(PAD + at, PAD), CONV), :].reshape(CONV // 8, 8, WIDE)
        for offset in by_shift:
            tap_sum[offset - 1] += jnp.sum(gated * moved(parts, offset), axis=0)
        tap_sum[KERNEL] += jnp.sum(gated, axis=0)
        return 0

    lax.fori_loop(0, seq_len // CONV, taps, 0)

    def sum_start(level, slots, mine, peers, value):
        slots[mine] = value
        for peer in peers:
            pltpu.make_async_remote_copy(
                src_ref=slots.at[mine],
                dst_ref=slots.at[mine],
                send_sem=sum_send.at[level],
                recv_sem=sum_recv.at[level],
                device_id={"dp": peer},
                device_id_type=MESH,
            ).start()

    def sum_end(level, slots, peers):
        whole = slots.at[pl.ds(0, len(peers))]
        pltpu.make_async_copy(whole, whole, sum_recv.at[level]).wait()
        value = slots[0]
        for i in range(1, len(peers) + 1):
            value = value + slots[i]
        return value

    sum_start(0, one, dp_core, core_peers, jnp.sum(tap_sum[...], axis=1))


    def key_step(step, _):
        step = far_first(step)
        columns = pl.ds(pl.multiple_of(step * ROWS, ROWS), ROWS)
        block = jnp.dot(q_t[0:HEAD, :], diffs[:, columns], preferred_element_type=F32)
        put(1, step, (block * back_scale).astype(BF16))
        return 0

    lax.fori_loop(0, steps, key_step, 0)
    sum_start(1, two, dp_x, x_peers, sum_end(0, one, core_peers))

    def collect(which, result):
        back[which, own_rows, :] = stage_out[which, own_rows, :]
        whole = back.at[which, others, :]
        pltpu.make_async_copy(whole, whole, recv_sem.at[out_sent[which]]).wait()
        for b in range(width // WIDE):
            result[0, :, b * WIDE : (b + 1) * WIDE] = back[which, b * WIDE : (b + 1) * WIDE, :].T

    collect(0, dq_ref)
    sum_start(2, three, dp_y, y_peers, sum_end(1, two, x_peers))
    collect(2, dv_ref)
    sums = sum_end(2, three, y_peers)
    dw_ref[...] = sums[0:KERNEL, 0:HEAD]
    db_ref[...] = sums[KERNEL : KERNEL + 1, 0:HEAD]
    collect(1, dk_ref)
    for i in range(1 if early else 0, len(landings) + 3):
        sent(i)
    for level, (slots, peers) in enumerate(((one, core_peers), (two, x_peers), (three, y_peers))):
        whole = slots.at[pl.ds(0, len(peers))]
        pltpu.make_async_copy(whole, whole, sum_send.at[level]).wait()


def on_device(queries, keys, values, grad_out, conv_weight, conv_bias, lengths):
    _, frames, width = queries.shape
    seq_len = frames * HEADS
    any_spec = pl.BlockSpec(memory_space=pl.ANY)
    vmem = pl.BlockSpec(memory_space=pltpu.VMEM)
    landing = pltpu.VMEM(queries.shape, BF16)
    tall = seq_len + 2 * PAD
    query_grad, key_grad, value_grad, weight_grad, bias_grad = pl.pallas_call(
        core,
        out_shape=(
            landing,
            landing,
            landing,
            jax.ShapeDtypeStruct((KERNEL, HEAD), F32),
            jax.ShapeDtypeStruct((1, HEAD), F32),
        ),
        in_specs=[any_spec] * 4 + [vmem, vmem, pl.BlockSpec(memory_space=pltpu.SMEM)],
        out_specs=(vmem,) * 5,
        scratch_shapes=[
            pltpu.VMEM((4, frames, width), BF16),
            pltpu.VMEM((4, width, frames), BF16),
            pltpu.VMEM((WIDE, seq_len), BF16),
            pltpu.VMEM((WIDE, seq_len), BF16),
            pltpu.VMEM((WIDE, seq_len), BF16),
            pltpu.VMEM((WIDE, seq_len), BF16),
            pltpu.VMEM((KERNEL + 1, 8, WIDE), F32),
            pltpu.VMEM((seq_len, seq_len), BF16),
            pltpu.VMEM((tall, WIDE), F32),
            pltpu.VMEM((seq_len, WIDE), F32),
            pltpu.VMEM((seq_len, WIDE), F32),
            pltpu.VMEM((tall, WIDE), F32),
            pltpu.VMEM((seq_len, WIDE), F32),
            pltpu.VMEM((seq_len, WIDE), BF16),
            pltpu.VMEM((WIDE, seq_len), BF16),
            pltpu.VMEM((seq_len, WIDE), F32),
            pltpu.VMEM((seq_len, WIDE), BF16),
            pltpu.VMEM((seq_len, seq_len), BF16),
            pltpu.VMEM((3, width, frames), BF16),
            pltpu.VMEM((3, width, frames), BF16),
            pltpu.VMEM((KERNEL + 1, 8, WIDE), F32),
            pltpu.VMEM((2, KERNEL + 1, WIDE), F32),
            pltpu.VMEM((4, KERNEL + 1, WIDE), F32),
            pltpu.VMEM((4, KERNEL + 1, WIDE), F32),
            pltpu.SemaphoreType.DMA((4, 4)),
            pltpu.SemaphoreType.DMA((4,)),
            pltpu.SemaphoreType.DMA((7,)),
            pltpu.SemaphoreType.DMA((7,)),
            pltpu.SemaphoreType.DMA((3, HEADS)),
            pltpu.SemaphoreType.DMA((3,)),
            pltpu.SemaphoreType.DMA((3,)),
        ],
        compiler_params=pltpu.CompilerParams(
            collective_id=0, has_side_effects=True, vmem_limit_bytes=56 << 20
        ),
    )(queries, keys, values, grad_out, conv_weight, conv_bias, lengths)
    return query_grad, key_grad, value_grad, weight_grad, bias_grad[0]


def solution(mesh):
    return jax.shard_map(
        on_device,
        mesh=mesh,
        in_specs=(
            P("dp", "seq", None),
            P("dp", "seq", None),
            P("dp", "seq", None),
            P("dp", "seq", None),
            P(),
            P(),
            P("dp"),
        ),
        out_specs=(
            P("dp", "seq", None),
            P("dp", "seq", None),
            P("dp", "seq", None),
            P(None, "seq"),
            P("seq"),
        ),
        check_vma=False,
    )
```
